32 devices in a mesh: tx: 4 (over y, x), ty: 8 (over z, core).
Axes of the slice: x: 2, y: 2, z: 4, core: 2. Of those that a mesh axis runs over, the one named last changes fastest.
Arguments:
- pressure: float32 [80, 64, 2048], P(None, 'tx', 'ty'), may hold values from -6 to 6
- velocity: float32 [3, 80, 64, 2048], P(None, None, 'tx', 'ty'), may hold values from -6 to 6
- kappa: float32 [80, 64, 2048], P(None, 'tx', 'ty'), may hold values from 0.05 to 0.5
- buoyancy: float32 [3, 80, 64, 2048], P(None, None, 'tx', 'ty'), may hold values from 0.1 to 1
- fwd_pressure: float32 [2, 80, 64, 2048], P(None, None, 'tx', 'ty'), may hold values from -6 to 6
- gradient: float32 [80, 64, 2048], P(None, 'tx', 'ty'), may hold values from -6 to 6
- traces: float32 [32768, 256], P(('tx', 'ty')), may hold values from -6 to 6
- kernel: float32 [2, 256], replicated, may hold values from -0.75 to 0.75
- rec_tile: int32 [32768, 1], P(('tx', 'ty')), may hold values from 0 to 31; in each aligned block of 1024 rows (0 to 1023, 1024 to 2047, ...) at most 64 rows name the same one
- rec_cell: int32 [32768], P(('tx', 'ty')), may hold values from 0 to 4095
Outputs:
- pressure_out: float32 [80, 64, 2048], P(None, 'tx', 'ty')
- velocity_out: float32 [3, 80, 64, 2048], P(None, None, 'tx', 'ty')
- gradient_out: float32 [80, 64, 2048], P(None, 'tx', 'ty')
The draws below stay inside these ranges and needn't reach their ends.
Inputs may be any that keep to these rules, and one draw needn't show every extreme that they name: `rec_tile`: in each aligned block of 1024 rows (the rows of one device) no tile is named by more than 64 rows, a bound that some block reaches.
All inputs are finite; a program needn't handle non-finite values.
Results may differ from the reference program's by a relative error of at most 0.00009.
Values sent between devices are 32-bit elements; how exact they have to be, the bound alone decides.
A program may use at most 128 MiB of HBM per device.

```python
import math
import jax
import jax.numpy as jnp
import numpy as np
from jax import lax

CX = 16
CY = 256
NZ = 80
NT = 256
STEPS = 2
REC_DEPTH = 3
R_DEV = 1024
CAP = 64
NX = 64
NY = 2048
NREC = 32768
N_TY = 8
DEVICES = 32


def place_ends(values, stream_key, low, high):
    dims = values.shape
    index_at = [jax.random.randint(jax.random.fold_in(stream_key, axis), (), 0, dims[axis]) for axis in range(len(dims))]
    values = values.at[tuple(index_at)].set(low)
    longest = dims.index(max(dims))
    index_at[longest] = (index_at[longest] + 1) % dims[longest]
    return values.at[tuple(index_at)].set(high)


def block_scale(own_key, extent, cuts, least, high):
    def one(axis_at, blocks):
        heights = jax.random.uniform(jax.random.fold_in(jax.random.fold_in(own_key, 6), axis_at), (blocks,), jnp.float32, least / len(cuts), high / len(cuts))
        return jnp.repeat(jnp.exp(heights), extent[axis_at] // blocks).reshape((-1,) + (1,) * (len(extent) - axis_at - 1))

    loudness = one(*cuts[0])
    for cut in cuts[1:]:
        loudness = loudness * one(*cut)
    return loudness


def routed_block(rng, own, number, rows, number_of, top, bound, lean):
    sequence = jax.random.permutation(rng, number_of)
    heavy_load, common = portions_of(number_of, rows * top, bound, lean, True), portions_of(number_of, rows * top, bound, lean, False)
    places = jnp.arange(number_of)

    def named(tallies, turn):
        used = int((tallies > 0).sum())
        fixed = max(1, used // 4)
        shifted = fixed + (places - fixed + turn * (used - fixed)) % max(1, number_of - fixed)
        return jnp.zeros((number_of,), jnp.int32).at[sequence[jnp.where(places < fixed, places, shifted)]].set(jnp.asarray(tallies, jnp.int32))

    tallies = jnp.where(number % 4 == 0, named(heavy_load, number // 4), named(common, number - number // 4 - 1))
    mixed = jax.random.permutation(jax.random.fold_in(own, 3), number_of)
    source_of, taker = mixed[0:number_of // 2 * 2:2], mixed[1:number_of // 2 * 2:2]
    slack = jnp.minimum(tallies[source_of] - 1, bound - tallies[taker]) // 2
    slack = jnp.where((source_of == sequence[0]) | (taker == sequence[0]) | (tallies[taker] == 0), 0, jnp.maximum(slack, 0))
    shifted = jax.random.randint(jax.random.fold_in(own, 4), (number_of // 2,), 0, 1 << 20) % (slack + 1)
    tallies = tallies.at[source_of].add(-shifted).at[taker].add(shifted)
    members = jnp.searchsorted(jnp.cumsum(tallies), jnp.arange(rows * top), side="right").astype(jnp.int32)
    listing = members.reshape(top, rows).T
    listing = listing[jax.random.permutation(jax.random.fold_in(own, 1), rows)]
    turn = jax.random.randint(jax.random.fold_in(own, 2), (rows, 1), 0, top)
    return jnp.take_along_axis(listing, (jnp.arange(top)[None, :] + turn) % top, axis=1)


def portions_of(number_of, total, reach, skew, full):
    loads = [(1 << 20) // math.isqrt(standing ** skew) + 1 for standing in range(1, number_of + 1)]
    largest = reach if full else min(reach, max(-(-total // number_of), total * loads[0] // sum(loads)))
    least = 1 if total - largest >= number_of - 1 else 0
    counts, rest = [largest] + [least] * (number_of - 1), total - largest - least * (number_of - 1)
    while rest > 0:
        candidates = [i for i in range(1, number_of) if counts[i] < largest] or [i for i in range(1, number_of) if counts[i] < reach]
        mass, remaining = sum([loads[i] for i in candidates]), rest
        for i in candidates:
            more = min(reach - counts[i], max(1, remaining * loads[i] // mass), rest)
            counts[i] = counts[i] + more
            rest = rest - more
    return np.array(counts)


def gaussian(stream_key, extent, deviation, bound, pieces=(), held_as=jnp.bfloat16):
    values = jax.random.normal(stream_key, extent, jnp.float32) * deviation
    if len(pieces) > 0:
        values = block_scale(stream_key, extent, pieces, -0.22, 0.18) * values
    return jnp.clip(values, min=-bound, max=bound).astype(held_as)


def setup_inputs(seed: int = 0) -> dict:
    key_of = jax.random.split(jax.random.key(seed), 11)
    pressure = gaussian(key_of[0], (NZ, NX, NY), 1.0, 6.0, ((1, 4), (2, 8)), jnp.float32)
    velocity = gaussian(key_of[1], (3, NZ, NX, NY), 1.0, 6.0, ((2, 4), (3, 8)), jnp.float32)
    kappa = jnp.clip(jnp.exp(math.log(0.5) - 2.3025851 * jax.random.uniform(key_of[2], (NZ, NX, NY), jnp.float32) ** block_scale(key_of[2], (NZ, NX, NY), ((1, 4), (2, 8)), -0.2, 0.2)), 0.05, 0.5)
    buoyancy = jnp.clip(jnp.exp(math.log(1.0) - 2.3025851 * jax.random.uniform(key_of[3], (3, NZ, NX, NY), jnp.float32) ** block_scale(key_of[3], (3, NZ, NX, NY), ((2, 4), (3, 8)), -0.2, 0.2)), 0.1, 1.0)
    fwd_pressure = gaussian(key_of[4], (STEPS, NZ, NX, NY), 1.0, 6.0, ((2, 4), (3, 8)), jnp.float32)
    gradient = gaussian(key_of[5], (NZ, NX, NY), 1.0, 6.0, ((1, 4), (2, 8)), jnp.float32)
    traces = gaussian(key_of[6], (NREC, NT), 1.0, 6.0, ((0, 32),), jnp.float32)
    kernel = gaussian(key_of[7], (STEPS, NT), (NT // 4) ** -0.5, 0.75, (), jnp.float32)
    rec_tile_keys = jax.random.split(jax.random.fold_in(key_of[8], 1), NREC // R_DEV)
    rec_tile_turns = jax.random.permutation(jax.random.fold_in(key_of[8], 3), NREC // R_DEV)
    rec_tile = jax.vmap(lambda own, number: routed_block(jax.random.fold_in(key_of[8], 2), own, number, R_DEV, DEVICES, 1, CAP, 2))(rec_tile_keys, rec_tile_turns).reshape((NREC, 1))
    rec_cell = place_ends(jax.random.randint(key_of[9], (NREC,), 0, CX * CY), jax.random.fold_in(key_of[9], 1), 0, (CX * CY) - 1).astype(jnp.int32)
    return {"pressure": pressure, "velocity": velocity, "kappa": kappa, "buoyancy": buoyancy, "fwd_pressure": fwd_pressure, "gradient": gradient, "traces": traces, "kernel": kernel, "rec_tile": rec_tile, "rec_cell": rec_cell}


coeffs = (1225.0 / 1024.0, -245.0 / 3072.0, 49.0 / 5120.0, -5.0 / 7168.0)


def along(field, axis, start, count):
    return lax.slice_in_dim(field, start, start + count, axis=axis)


def plus_diff(field, axis, count):
    total = coeffs[0] * (along(field, axis, 5, count) - along(field, axis, 4, count))
    for k in range(2, 5):
        total = total + coeffs[k - 1] * (along(field, axis, 4 + k, count) - along(field, axis, 5 - k, count))
    return total


def minus_diff(field, axis, count):
    total = coeffs[0] * (along(field, axis, 4, count) - along(field, axis, 3, count))
    for k in range(2, 5):
        total = total + coeffs[k - 1] * (along(field, axis, 3 + k, count) - along(field, axis, 4 - k, count))
    return total


def reference(pressure, velocity, kappa, buoyancy, fwd_pressure, gradient, traces, kernel, rec_tile, rec_cell):
    nz, nx, ny = pressure.shape
    tiles = rec_tile[:, 0]
    gx = (tiles // N_TY) * CX + rec_cell // CY
    gy = (tiles % N_TY) * CY + rec_cell % CY
    flat = (gx * ny + gy).astype(jnp.int32)
    sources = jnp.einsum("sk,rk->sr", kernel, traces, precision=lax.Precision.HIGHEST)
    inject = jax.ops.segment_sum(sources.T, flat, num_segments=nx * ny)
    inject = inject.T.reshape(STEPS, nx, ny)
    press = pressure
    vel_x, vel_y, vel_z = velocity[0], velocity[1], velocity[2]
    grad = gradient
    for step in range(STEPS):
        padded = jnp.pad(press, ((0, 0), (4, 4), (4, 4)))
        vel_x = vel_x - buoyancy[0] * plus_diff(padded[:, :, 4:4 + ny], 1, nx)
        vel_y = vel_y - buoyancy[1] * plus_diff(padded[:, 4:4 + nx, :], 2, ny)
        zpadded = jnp.pad(press, ((4, 4), (0, 0), (0, 0)))
        vel_z = vel_z - buoyancy[2] * plus_diff(zpadded, 0, nz)
        xpad = jnp.pad(vel_x, ((0, 0), (4, 4), (0, 0)))
        ypad = jnp.pad(vel_y, ((0, 0), (0, 0), (4, 4)))
        zpad = jnp.pad(vel_z, ((4, 4), (0, 0), (0, 0)))
        diverge = minus_diff(xpad, 1, nx) + minus_diff(ypad, 2, ny) + minus_diff(zpad, 0, nz)
        press = press - kappa * diverge
        press = press.at[REC_DEPTH].add(inject[step])
        grad = grad + fwd_pressure[step] * press
    return press, jnp.stack([vel_x, vel_y, vel_z]), grad
```

```python
import functools

import jax
import jax.numpy as jnp
import ml_dtypes
import numpy as np
from jax import lax
from jax.experimental import pallas as pl
from jax.experimental.pallas import tpu as pltpu
from jax.sharding import PartitionSpec as P

STEPS = 2
REC_DEPTH = 3
ZC = 16
MESH = pl.DeviceIdType.MESH
F32 = jnp.float32
BF16 = jnp.bfloat16

coeffs = (1225.0 / 1024.0, -245.0 / 3072.0, 49.0 / 5120.0, -5.0 / 7168.0)


def tap(offset, plus):
    for k in range(1, 5):
        if offset == (k if plus else k - 1):
            return coeffs[k - 1]
        if offset == (1 - k if plus else -k):
            return -coeffs[k - 1]
    return 0.0


def band(outs, ins, plus):
    return np.array([[tap(i - o, plus) for i in ins] for o in outs], np.float64)


def parts(m):
    m = np.asarray(m, np.float32)
    hi = m.astype(ml_dtypes.bfloat16)
    lo = (m - hi.astype(np.float32)).astype(ml_dtypes.bfloat16)
    return hi, lo


def x_matrix(cx, plus):
    eye = np.eye(ZC)
    low, up = (3, 4) if plus else (4, 3)
    own = np.kron(eye, band(range(cx), range(cx), plus))
    below = np.kron(eye, band(range(cx), range(-low, 0), plus))
    above = np.kron(eye, band(range(cx), range(cx, cx + up), plus))
    oh, ol = parts(own)
    hh, hl = parts(np.concatenate([below, above], axis=1))
    pad = np.zeros((ZC * cx, 48), ml_dtypes.bfloat16)
    return np.concatenate([oh, oh, ol, hh, hh, hl, pad], axis=1)


def y_matrix(cy, plus):
    own = band(range(cy), range(cy), plus).T
    halo = band(range(cy), list(range(-8, 0)) + list(range(cy, cy + 8)), plus).T
    oh, ol = parts(own)
    hh, hl = parts(halo)
    pad = np.zeros((80, cy), ml_dtypes.bfloat16)
    return np.concatenate([oh, oh, ol, hh, hh, hl, pad], axis=0)


def x_edges(cx, plus):
    low, up = (3, 4) if plus else (4, 3)
    eye = np.eye(ZC)
    to_up = np.kron(eye, np.eye(cx)[cx - low:])
    to_low = np.kron(eye, np.eye(cx)[:up])
    pick = np.concatenate([to_up, to_low], axis=0).astype(ml_dtypes.bfloat16)
    return np.concatenate([pick, pick], axis=1)


def y_edges(cy):
    eye = np.eye(cy)
    pick = np.concatenate([eye[cy - 8:], eye[:8]], axis=0).astype(ml_dtypes.bfloat16)
    return np.concatenate([pick, pick], axis=1)


def split(v):
    hi = v.astype(BF16)
    return hi, (v - hi.astype(F32)).astype(BF16)


def dot(a, b):
    return lax.dot_general(a, b, (((1,), (0,)), ((), ())), preferred_element_type=F32)


def dot_nt(a, b):
    return lax.dot_general(a, b, (((1,), (1,)), ((), ())), preferred_element_type=F32)


def route_kernel(devices, slots, traces_ref, kernel_ref, tile_ref, cell_ref, out_ref):
    rows = traces_ref.shape[0]
    src = lax.dot_general(
        kernel_ref[...], traces_ref[...], (((1,), (1,)), ((), ())),
        precision=lax.Precision.HIGHEST, preferred_element_type=F32)
    tiles = tile_ref[...]
    cells = cell_ref[...]
    named = lax.broadcasted_iota(jnp.int32, (devices, rows), 0) == tiles
    onehot = jnp.where(named, 1.0, 0.0)
    earlier = (lax.broadcasted_iota(jnp.int32, (rows, rows), 0)
               < lax.broadcasted_iota(jnp.int32, (rows, rows), 1))
    count = dot(onehot.astype(BF16), jnp.where(earlier, 1.0, 0.0).astype(BF16))
    rank = jnp.sum(count * onehot, axis=0, keepdims=True)
    slot_id = lax.broadcasted_iota(jnp.int32, (slots, rows), 0).astype(F32)
    place = jnp.where(slot_id == rank, 1.0, 0.0).astype(BF16)
    hi = src.astype(BF16).astype(F32)
    lo = src - hi
    cell_x = (cells // 256).astype(F32)
    cell_y = (cells % 256).astype(F32)
    vals = [hi[0:1], lo[0:1], hi[1:2], lo[1:2], cell_x, cell_y]
    lhs = jnp.concatenate([(onehot * v).astype(BF16) for v in vals], axis=0)
    packed = dot_nt(lhs, place)
    d = devices
    out_ref[0] = packed[0:d] + packed[d:2 * d]
    out_ref[1] = packed[2 * d:3 * d] + packed[3 * d:4 * d]
    out_ref[2] = packed[4 * d:5 * d] * 256.0 + packed[5 * d:6 * d]


def step_kernel(n_tx, n_ty, nz, cx, cy,
                p_in, v_in, kap_in, b_in, fwd_in, g_in, recv_in,
                xp_in, xm_in, yp_in, ym_in, sxp_in, sxm_in, sy_in,
                p_out, v_out, g_out,
                p, vx, vy, vz, kap, buo, fwd, grad,
                xp, xm, yp, ym, sxp, sxm, sy,
                xs, xr, ys, yr, inj,
                in_sem, out_sem, send_sem, recv_sem):
    tx, ty = lax.axis_index("tx"), lax.axis_index("ty")
    rows = nz * cx
    cr = ZC * cx
    pad = 4 * cx
    n_chunks = rows // cr
    has = (tx < n_tx - 1, tx > 0, ty < n_ty - 1, ty > 0)
    ids = ({"tx": tx + 1}, {"tx": tx - 1}, {"ty": ty + 1}, {"ty": ty - 1})
    back = (1, 0, 3, 2)

    body = pl.ds(pad, rows)
    loads = [
        pltpu.make_async_copy(p_in, p.at[body], in_sem.at[0]),
        pltpu.make_async_copy(sxp_in, sxp, in_sem.at[1]),
        pltpu.make_async_copy(sy_in, sy, in_sem.at[2]),
        pltpu.make_async_copy(xp_in, xp, in_sem.at[3]),
        pltpu.make_async_copy(yp_in, yp, in_sem.at[4]),
        pltpu.make_async_copy(v_in.at[0], vx, in_sem.at[5]),
        pltpu.make_async_copy(v_in.at[1], vy, in_sem.at[6]),
        pltpu.make_async_copy(v_in.at[2], vz.at[body], in_sem.at[7]),
        pltpu.make_async_copy(b_in, buo, in_sem.at[8]),
        pltpu.make_async_copy(sxm_in, sxm, in_sem.at[9]),
        pltpu.make_async_copy(xm_in, xm, in_sem.at[10]),
        pltpu.make_async_copy(ym_in, ym, in_sem.at[11]),
        pltpu.make_async_copy(kap_in, kap, in_sem.at[12]),
        pltpu.make_async_copy(fwd_in, fwd, in_sem.at[13]),
        pltpu.make_async_copy(g_in, grad, in_sem.at[14]),
    ]
    for copy in loads:
        copy.start()

    zeros = jnp.zeros((pad, cy), F32)
    for ref in (p, vz):
        ref[0:pad, :] = zeros
        ref[pad + rows:, :] = zeros

    def span(ph, d):
        low, up = (3 * ZC, 4 * ZC) if ph % 2 == 0 else (4 * ZC, 3 * ZC)
        return ((0, low), (low, up), (0, 8), (8, 8))[d]

    def clear(d):
        @pl.when(jnp.logical_not(has[back[d]]))
        def _():
            for ph in range(4):
                start, size = span(ph, d)
                ref = xr if d < 2 else yr
                for c in range(n_chunks):
                    ref[ph, c, start:start + size, :] = jnp.zeros((size, ref.shape[3]), F32)

    for d in range(4):
        clear(d)

    barrier = pltpu.get_barrier_semaphore()
    for d in range(4):
        @pl.when(has[d])
        def _(d=d):
            pl.semaphore_signal(barrier, inc=1, device_id=ids[d], device_id_type=MESH)
    peers = sum(h.astype(jnp.int32) for h in has)
    pl.semaphore_wait(barrier, peers)

    def halo_copy(ph, c, d):
        start, size = span(ph, d)
        src, dst = (xs, xr) if d < 2 else (ys, yr)
        return pltpu.make_async_remote_copy(
            src_ref=src.at[ph, c, pl.ds(start, size)],
            dst_ref=dst.at[ph, c, pl.ds(start, size)],
            send_sem=send_sem.at[ph, c, d],
            recv_sem=recv_sem.at[ph, c, d],
            device_id=ids[d], device_id_type=MESH)

    def send(ph, c):
        for d in range(4):
            @pl.when(has[d])
            def _(d=d):
                halo_copy(ph, c, d).start()

    def arrive(ph, c):
        for d in range(4):
            @pl.when(has[back[d]])
            def _(d=d):
                start, size = span(ph, d)
                src, dst = (xs, xr) if d < 2 else (ys, yr)
                pltpu.make_async_remote_copy(
                    src_ref=src.at[ph, c, pl.ds(start, size)],
                    dst_ref=dst.at[ph, c, pl.ds(start, size)],
                    send_sem=send_sem.at[ph, c, d],
                    recv_sem=recv_sem.at[ph, c, d],
                    device_id=ids[back[d]], device_id_type=MESH).wait_recv()

    def post(ph, c, pick, fx, fy):
        hi, lo = split(fx)
        xs[ph, c] = dot(pick[...], jnp.concatenate([hi, lo], axis=0))
        hi, lo = split(fy)
        ys[ph, c] = dot_nt(sy[...], jnp.concatenate([hi, lo], axis=1))
        send(ph, c)

    def x_diff(ph, c, field, matrix):
        hi, lo = split(field)
        hh, hl = split(xr[ph, c])
        tail = jnp.zeros((48, cy), BF16)
        return dot(matrix[...], jnp.concatenate([hi, lo, hi, hh, hl, hh, tail], axis=0))

    def y_diff(ph, c, field, matrix):
        hi, lo = split(field)
        hh, hl = split(yr[ph, c])
        hh, hl = hh.astype(F32), hl.astype(F32)
        halo = jnp.concatenate([hh, hl, hh, jnp.zeros((80, cr), F32)], axis=0)
        return dot(jnp.concatenate([hi, lo, hi, halo.T.astype(BF16)], axis=1), matrix[...])

    def z_diff(ref, c, plus):
        total = None
        for k in range(1, 5):
            a, b = (k, 1 - k) if plus else (k - 1, -k)
            fa = ref[pl.ds(pl.multiple_of(c * cr + (pad + a * cx), 8), cr), :]
            fb = ref[pl.ds(pl.multiple_of(c * cr + (pad + b * cx), 8), cr), :]
            term = coeffs[k - 1] * (fa - fb)
            total = term if total is None else total + term
        return total

    def at(c):
        return pl.ds(pl.multiple_of(c * cr, cr), cr)

    def padded_at(c):
        return pl.ds(pl.multiple_of(c * cr + pad, 8), cr)

    for i in range(3):
        loads[i].wait()

    @pl.loop(0, n_chunks)
    def _(c):
        f = p[padded_at(c), :]
        post(0, c, sxp, f, f)

    slots_all = recv_in.shape[1]
    piece = 512
    total = jnp.zeros((4 * cx, cy), F32)
    for r in range(slots_all // piece):
        got = recv_in[:, r * piece:(r + 1) * piece]
        cell = got[2:3].astype(jnp.int32)
        at_x = lax.broadcasted_iota(jnp.int32, (cx, piece), 0) == cell // cy
        at_y = lax.broadcasted_iota(jnp.int32, (cy, piece), 0) == cell % cy
        pieces = []
        for s in range(STEPS):
            v = got[s:s + 1]
            hi = v.astype(BF16).astype(F32)
            pieces.append(jnp.where(at_x, hi, 0.0).astype(BF16))
            pieces.append(jnp.where(at_x, v - hi, 0.0).astype(BF16))
        total = total + dot_nt(jnp.concatenate(pieces, axis=0),
                               jnp.where(at_y, 1.0, 0.0).astype(BF16))
    for s in range(STEPS):
        inj[s] = total[2 * s * cx:(2 * s + 1) * cx] + total[(2 * s + 1) * cx:(2 * s + 2) * cx]

    for i in range(3, 10):
        loads[i].wait()

    for s in range(STEPS):
        @pl.loop(0, n_chunks)
        def _(c, s=s):
            vz[padded_at(c), :] = vz[padded_at(c), :] - buo[2, at(c), :] * z_diff(p, c, True)
            arrive(2 * s, c)
            f = p[padded_at(c), :]
            nx = vx[at(c), :] - buo[0, at(c), :] * x_diff(2 * s, c, f, xp)
            vx[at(c), :] = nx
            ny = vy[at(c), :] - buo[1, at(c), :] * y_diff(2 * s, c, f, yp)
            vy[at(c), :] = ny
            post(2 * s + 1, c, sxm, nx, ny)

        if s == 0:
            for i in range(10, 15):
                loads[i].wait()
        if s == STEPS - 1:
            outs = [
                pltpu.make_async_copy(vx, v_out.at[0], out_sem.at[0]),
                pltpu.make_async_copy(vy, v_out.at[1], out_sem.at[1]),
                pltpu.make_async_copy(vz.at[body], v_out.at[2], out_sem.at[2]),
            ]
            for copy in outs:
                copy.start()

        @pl.loop(0, n_chunks)
        def _(c, s=s):
            dz = z_diff(vz, c, False)
            arrive(2 * s + 1, c)
            div = (x_diff(2 * s + 1, c, vx[at(c), :], xm)
                   + y_diff(2 * s + 1, c, vy[at(c), :], ym) + dz)
            p[padded_at(c), :] = p[padded_at(c), :] - kap[at(c), :] * div

            @pl.when(c == REC_DEPTH // ZC)
            def _():
                row = pad + REC_DEPTH * cx
                p[row:row + cx, :] = p[row:row + cx, :] + inj[s]

            f = p[padded_at(c), :]
            grad[at(c), :] = grad[at(c), :] + fwd[s, at(c), :] * f
            if s < STEPS - 1:
                post(2 * s + 2, c, sxp, f, f)

    last = [
        pltpu.make_async_copy(p.at[body], p_out, out_sem.at[3]),
        pltpu.make_async_copy(grad, g_out, out_sem.at[4]),
    ]
    for copy in last:
        copy.start()

    @pl.loop(0, n_chunks)
    def _(c):
        for ph in range(4):
            for d in range(4):
                @pl.when(has[d])
                def _(ph=ph, d=d):
                    halo_copy(ph, c, d).wait_send()

    for copy in outs + last:
        copy.wait()


def local(
    pressure, velocity, kappa, buoyancy, fwd_pressure, gradient, traces, kernel, rec_tile, rec_cell
):
    nz, cx, cy = pressure.shape
    n_rows, samples = traces.shape
    n_tx, n_ty = lax.axis_size("tx"), lax.axis_size("ty")
    devices = n_tx * n_ty
    slots = max(4, 2 * n_rows // devices)
    vmem = pl.BlockSpec(memory_space=pltpu.VMEM)
    anywhere = pl.BlockSpec(memory_space=pl.ANY)

    packed = pl.pallas_call(
        functools.partial(route_kernel, devices, slots),
        out_shape=jax.ShapeDtypeStruct((3, devices, slots), F32),
        in_specs=[vmem] * 4,
        out_specs=vmem,
        compiler_params=pltpu.CompilerParams(vmem_limit_bytes=32 * 2**20),
        name="route",
    )(traces, kernel, rec_tile.reshape(1, n_rows), rec_cell.reshape(1, n_rows))
    got = lax.all_to_all(packed, ("tx", "ty"), split_axis=1, concat_axis=1, tiled=True)
    got = got.reshape(3, devices * slots)

    rows = nz * cx
    cr = ZC * cx
    nc = rows // cr
    pad = 4 * cx
    flat = lambda a: a.reshape(a.shape[:-3] + (rows, cy))
    mats = [x_matrix(cx, True), x_matrix(cx, False), y_matrix(cy, True), y_matrix(cy, False),
            x_edges(cx, True), x_edges(cx, False), y_edges(cy)]
    field = lambda *lead: pltpu.VMEM(lead + (rows, cy), F32)
    press, vel, grad = pl.pallas_call(
        functools.partial(step_kernel, n_tx, n_ty, nz, cx, cy),
        out_shape=(jax.ShapeDtypeStruct((rows, cy), F32),
                   jax.ShapeDtypeStruct((3, rows, cy), F32),
                   jax.ShapeDtypeStruct((rows, cy), F32)),
        in_specs=[anywhere] * 6 + [vmem] + [anywhere] * 7,
        out_specs=(anywhere,) * 3,
        scratch_shapes=[
            pltpu.VMEM((rows + 2 * pad, cy), F32), field(), field(),
            pltpu.VMEM((rows + 2 * pad, cy), F32), field(), field(3), field(STEPS), field(),
        ] + [pltpu.VMEM(m.shape, BF16) for m in mats] + [
            pltpu.VMEM((4, nc, 7 * ZC, cy), F32), pltpu.VMEM((4, nc, 7 * ZC, cy), F32),
            pltpu.VMEM((4, nc, 16, cr), F32), pltpu.VMEM((4, nc, 16, cr), F32),
            pltpu.VMEM((STEPS, cx, cy), F32),
            pltpu.SemaphoreType.DMA((15,)), pltpu.SemaphoreType.DMA((5,)),
            pltpu.SemaphoreType.DMA((4, nc, 4)), pltpu.SemaphoreType.DMA((4, nc, 4)),
        ],
        compiler_params=pltpu.CompilerParams(
            collective_id=0, has_side_effects=True, vmem_limit_bytes=48 * 2**20),
        name="steps",
    )(flat(pressure), flat(velocity), flat(kappa), flat(buoyancy), flat(fwd_pressure),
      flat(gradient), got, *[jnp.asarray(m) for m in mats])
    return (press.reshape(nz, cx, cy), vel.reshape(3, nz, cx, cy), grad.reshape(nz, cx, cy))


def solution(mesh):
    return jax.shard_map(
        local,
        mesh=mesh,
        in_specs=(
            P(None, "tx", "ty"),
            P(None, None, "tx", "ty"),
            P(None, "tx", "ty"),
            P(None, None, "tx", "ty"),
            P(None, None, "tx", "ty"),
            P(None, "tx", "ty"),
            P(("tx", "ty"), None),
            P(),
            P(("tx", "ty"), None),
            P(("tx", "ty")),
        ),
        out_specs=(P(None, "tx", "ty"), P(None, None, "tx", "ty"), P(None, "tx", "ty")),
        check_vma=False,
    )
```

```python
import functools

import jax
import jax.numpy as jnp
import ml_dtypes
import numpy as np
from jax import lax
from jax.experimental import pallas as pl
from jax.experimental.pallas import tpu as pltpu
from jax.sharding import PartitionSpec as P

STEPS = 2
REC_DEPTH = 3
ZC = 16
MESH = pl.DeviceIdType.MESH
F32 = jnp.float32
BF16 = jnp.bfloat16

coeffs = (1225.0 / 1024.0, -245.0 / 3072.0, 49.0 / 5120.0, -5.0 / 7168.0)


def tap(offset, plus):
    for k in range(1, 5):
        if offset == (k if plus else k - 1):
            return coeffs[k - 1]
        if offset == (1 - k if plus else -k):
            return -coeffs[k - 1]
    return 0.0


def taps(offset, plus):
    hi = jnp.zeros(offset.shape, F32)
    lo = jnp.zeros(offset.shape, F32)
    for at in range(-4, 5):
        c = tap(at, plus)
        if c != 0.0:
            c_hi = float(np.float32(c).astype(ml_dtypes.bfloat16))
            hi = jnp.where(offset == at, c_hi, hi)
            lo = jnp.where(offset == at, float(np.float32(c)) - c_hi, lo)
    return hi, lo


def grid_of(shape):
    return (lax.broadcasted_iota(jnp.int32, shape, 0), lax.broadcasted_iota(jnp.int32, shape, 1))


FAR = 1 << 20


def build_x(ref, cx, plus):
    cr = ZC * cx
    low = 3 if plus else 4
    row, col = grid_of((cr, cr))
    hi, lo = taps(jnp.where(row // cx == col // cx, col % cx - row % cx, FAR), plus)
    ref[:, 0:cr] = hi.astype(BF16)
    ref[:, cr:2 * cr] = hi.astype(BF16)
    ref[:, 2 * cr:3 * cr] = lo.astype(BF16)
    width = 7 * ZC
    row, col = grid_of((cr, ref.shape[1] - 3 * cr))
    seg = jnp.where(col < width, 0, jnp.where(col < 2 * width, 1, jnp.where(col < 3 * width, 2, 3)))
    at = col - seg * width
    layer = at // ZC
    x = jnp.where(layer < low, layer - low, cx + layer - low)
    hi, lo = taps(jnp.where(row // cx == at % ZC, x - row % cx, FAR), plus)
    ref[:, 3 * cr:] = jnp.where(seg < 2, hi, jnp.where(seg == 2, lo, 0.0)).astype(BF16)


def build_y(ref, cy, plus):
    row, col = grid_of((cy, cy))
    hi, lo = taps(row - col, plus)
    ref[0:cy] = hi.astype(BF16)
    ref[cy:2 * cy] = hi.astype(BF16)
    ref[2 * cy:3 * cy] = lo.astype(BF16)
    row, col = grid_of((ref.shape[0] - 3 * cy, cy))
    seg, at = row // 16, row % 16
    hi, lo = taps(jnp.where(at < 8, at - 8, cy + at - 8) - col, plus)
    ref[3 * cy:] = jnp.where(seg < 2, hi, jnp.where(seg == 2, lo, 0.0)).astype(BF16)


def build_x_edges(ref, cx, plus):
    low = 3 if plus else 4
    row, col = grid_of(ref.shape)
    at = col % (ZC * cx)
    layer = row // ZC
    x = jnp.where(layer < low, cx - low + layer, layer - low)
    ref[...] = jnp.where(at == (row % ZC) * cx + x, 1.0, 0.0).astype(BF16)


def build_y_edges(ref, cy):
    row, col = grid_of(ref.shape)
    ref[...] = jnp.where(col % cy == jnp.where(row < 8, cy - 8 + row, row - 8), 1.0, 0.0).astype(BF16)


def split(v):
    hi = v.astype(BF16)
    return hi, (v - hi.astype(F32)).astype(BF16)


def dot(a, b):
    return lax.dot_general(a, b, (((1,), (0,)), ((), ())), preferred_element_type=F32)


def dot_nt(a, b):
    return lax.dot_general(a, b, (((1,), (1,)), ((), ())), preferred_element_type=F32)


def pack(devices, traces, kernel, tiles, cells):
    rows = traces.shape[0]
    src = lax.dot_general(
        kernel, traces, (((1,), (1,)), ((), ())),
        precision=lax.Precision.HIGHEST, preferred_element_type=F32)
    named = lax.broadcasted_iota(jnp.int32, (devices, rows), 0) == tiles
    onehot = jnp.where(named, 1.0, 0.0)
    row, col = grid_of((rows, rows))
    count = dot(onehot.astype(BF16), jnp.where(row < col, 1.0, 0.0).astype(BF16))
    rank = jnp.sum(count * onehot, axis=0, keepdims=True)
    slot_id = lax.broadcasted_iota(jnp.int32, (128, rows), 0).astype(F32)
    place = jnp.where(slot_id == rank, 1.0, 0.0).astype(BF16)
    src_hi = src.astype(BF16).astype(F32)
    cell_lo = cells % 256
    none = jnp.zeros((5, rows), F32)
    hi = jnp.concatenate([src_hi, (cells - cell_lo).astype(F32), none], axis=0)
    lo = jnp.concatenate([src - src_hi, cell_lo.astype(F32), none], axis=0)
    packed = None
    for v in (hi, lo):
        spread = jnp.concatenate([v] * devices, axis=0)
        to = lax.broadcasted_iota(jnp.int32, (devices * 8, rows), 0) // 8 == tiles
        part = dot_nt(jnp.where(to, spread, 0.0).astype(BF16), place)
        packed = part if packed is None else packed + part
    return packed.reshape(devices, 8, 128)


def step_kernel(n_tx, n_ty, nz, cx, cy,
                p_in, v_in, kap_in, b_in, fwd_in, g_in, traces_in, kernel_in, tile_in, cell_in,
                p_out, v_out, g_out,
                p, vx, vy, vz, kap, buo, fwd, grad, traces, filt, tiles, cells,
                xp, xm, yp, ym, sxp, sxm, sy,
                xs, xr, ys, yr, ts, tr, inj,
                in_sem, out_sem, send_sem, recv_sem, to_sem, from_sem):
    tx, ty = lax.axis_index("tx"), lax.axis_index("ty")
    devices = n_tx * n_ty
    me = tx * n_ty + ty
    rows = nz * cx
    cr = ZC * cx
    pad = 4 * cx
    n_chunks = rows // cr
    has = (tx < n_tx - 1, tx > 0, ty < n_ty - 1, ty > 0)
    ids = ({"tx": tx + 1}, {"tx": tx - 1}, {"ty": ty + 1}, {"ty": ty - 1})
    back = (1, 0, 3, 2)

    body = pl.ds(pad, rows)
    pairs = [
        (p_in, p.at[body]), (traces_in, traces), (kernel_in, filt), (tile_in, tiles),
        (cell_in, cells), (v_in.at[0], vx), (v_in.at[1], vy), (v_in.at[2], vz.at[body]),
        (b_in, buo), (kap_in, kap), (fwd_in, fwd), (g_in, grad),
    ]
    loads = [pltpu.make_async_copy(a, b, in_sem.at[i]) for i, (a, b) in enumerate(pairs)]
    for copy in loads:
        copy.start()

    barrier = pltpu.get_barrier_semaphore()

    def peer(o):
        to = lax.rem(me + o, devices)
        return to, {"tx": to // n_ty, "ty": lax.rem(to, n_ty)}

    @pl.loop(1, devices)
    def _(o):
        pl.semaphore_signal(barrier, inc=1, device_id=peer(o)[1], device_id_type=MESH)

    zeros = jnp.zeros((pad, cy), F32)
    for ref in (p, vz):
        ref[0:pad, :] = zeros
        ref[pad + rows:, :] = zeros

    def span(ph, d):
        low, up = (3 * ZC, 4 * ZC) if ph % 2 == 0 else (4 * ZC, 3 * ZC)
        return ((0, low), (low, up), (0, 8), (8, 8))[d]

    def clear(d):
        @pl.when(jnp.logical_not(has[back[d]]))
        def _():
            for ph in range(4):
                start, size = span(ph, d)
                ref = xr if d < 2 else yr
                for c in range(n_chunks):
                    ref[ph, c, start:start + size, :] = jnp.zeros((size, ref.shape[3]), F32)

    for d in range(4):
        clear(d)

    build_x_edges(sxp, cx, True)
    build_y_edges(sy, cy)
    pl.semaphore_wait(barrier, devices - 1)

    def halo_copy(ph, c, d):
        start, size = span(ph, d)
        src, dst = (xs, xr) if d < 2 else (ys, yr)
        return pltpu.make_async_remote_copy(
            src_ref=src.at[ph, c, pl.ds(start, size)],
            dst_ref=dst.at[ph, c, pl.ds(start, size)],
            send_sem=send_sem.at[ph, c, d],
            recv_sem=recv_sem.at[ph, c, d],
            device_id=ids[d], device_id_type=MESH)

    def send(ph, c):
        for d in range(4):
            @pl.when(has[d])
            def _(d=d):
                halo_copy(ph, c, d).start()

    def arrive(ph, c):
        for d in range(4):
            @pl.when(has[back[d]])
            def _(d=d):
                start, size = span(ph, d)
                src, dst = (xs, xr) if d < 2 else (ys, yr)
                pltpu.make_async_remote_copy(
                    src_ref=src.at[ph, c, pl.ds(start, size)],
                    dst_ref=dst.at[ph, c, pl.ds(start, size)],
                    send_sem=send_sem.at[ph, c, d],
                    recv_sem=recv_sem.at[ph, c, d],
                    device_id=ids[back[d]], device_id_type=MESH).wait_recv()

    def post(ph, c, pick, fx, fy):
        hi, lo = split(fx)
        xs[ph, c] = dot(pick[...], jnp.concatenate([hi, lo], axis=0))
        hi, lo = split(fy)
        ys[ph, c] = dot_nt(sy[...], jnp.concatenate([hi, lo], axis=1))
        send(ph, c)

    def x_diff(ph, c, field, matrix):
        hi, lo = split(field)
        hh, hl = split(xr[ph, c])
        tail = jnp.zeros((48, cy), BF16)
        return dot(matrix[...], jnp.concatenate([hi, lo, hi, hh, hl, hh, tail], axis=0))

    def y_diff(ph, c, field, matrix):
        hi, lo = split(field)
        hh, hl = split(yr[ph, c])
        hh, hl = hh.astype(F32), hl.astype(F32)
        halo = jnp.concatenate([hh, hl, hh, jnp.zeros((80, cr), F32)], axis=0)
        return dot(jnp.concatenate([hi, lo, hi, halo.T.astype(BF16)], axis=1), matrix[...])

    def z_diff(ref, c, plus):
        total = None
        for k in range(1, 5):
            a, b = (k, 1 - k) if plus else (k - 1, -k)
            fa = ref[pl.ds(pl.multiple_of(c * cr + (pad + a * cx), 8), cr), :]
            fb = ref[pl.ds(pl.multiple_of(c * cr + (pad + b * cx), 8), cr), :]
            term = coeffs[k - 1] * (fa - fb)
            total = term if total is None else total + term
        return total

    def at(c):
        return pl.ds(pl.multiple_of(c * cr, cr), cr)

    def padded_at(c):
        return pl.ds(pl.multiple_of(c * cr + pad, 8), cr)

    loads[0].wait()

    @pl.loop(0, n_chunks)
    def _(c):
        f = p[padded_at(c), :]
        post(0, c, sxp, f, f)

    def trace_copy(o):
        to, place = peer(o)
        return pltpu.make_async_remote_copy(
            src_ref=ts.at[to], dst_ref=tr.at[o],
            send_sem=to_sem.at[o], recv_sem=from_sem.at[o],
            device_id=place, device_id_type=MESH)

    for i in range(1, 5):
        loads[i].wait()
    ts[...] = pack(devices, traces[...], filt[...], tiles[...], cells[...])

    @pl.loop(1, devices)
    def _(o):
        trace_copy(o).start()

    tr[0] = ts[me]
    build_x(xp, cx, True)
    build_y(yp, cy, True)
    build_x_edges(sxm, cx, False)
    for i in range(5, 9):
        loads[i].wait()

    def receive():
        @pl.loop(1, devices)
        def _(o):
            trace_copy(o).wait_recv()

        def gather(i, total):
            got = jnp.concatenate([tr[4 * i + j] for j in range(4)], axis=1)
            cell = got[2:3].astype(jnp.int32)
            at_x = lax.broadcasted_iota(jnp.int32, (cx, 512), 0) == cell // cy
            at_y = lax.broadcasted_iota(jnp.int32, (cy, 512), 0) == cell % cy
            pieces = []
            for s in range(STEPS):
                v = got[s:s + 1]
                hi = v.astype(BF16).astype(F32)
                pieces.append(jnp.where(at_x, hi, 0.0).astype(BF16))
                pieces.append(jnp.where(at_x, v - hi, 0.0).astype(BF16))
            return total + dot_nt(jnp.concatenate(pieces, axis=0),
                                  jnp.where(at_y, 1.0, 0.0).astype(BF16))

        total = lax.fori_loop(0, devices // 4, gather, jnp.zeros((4 * cx, cy), F32))
        for s in range(STEPS):
            inj[s] = total[2 * s * cx:(2 * s + 1) * cx] + total[(2 * s + 1) * cx:(2 * s + 2) * cx]

    for s in range(STEPS):
        @pl.loop(0, n_chunks)
        def _(c, s=s):
            nz_new = vz[padded_at(c), :] - buo[2, at(c), :] * z_diff(p, c, True)
            vz[padded_at(c), :] = nz_new
            arrive(2 * s, c)
            f = p[padded_at(c), :]
            nx = vx[at(c), :] - buo[0, at(c), :] * x_diff(2 * s, c, f, xp)
            vx[at(c), :] = nx
            ny = vy[at(c), :] - buo[1, at(c), :] * y_diff(2 * s, c, f, yp)
            vy[at(c), :] = ny
            post(2 * s + 1, c, sxm, nx, ny)

        if s == 0:
            build_x(xm, cx, False)
            build_y(ym, cy, False)
            receive()
            for i in range(9, 12):
                loads[i].wait()

        if s == STEPS - 1:
            outs = [
                pltpu.make_async_copy(vx, v_out.at[0], out_sem.at[0, 2]),
                pltpu.make_async_copy(vy, v_out.at[1], out_sem.at[1, 2]),
                pltpu.make_async_copy(vz.at[body], v_out.at[2], out_sem.at[2, 2]),
            ]
            for copy in outs:
                copy.start()

        def result(c):
            return (pltpu.make_async_copy(p.at[padded_at(c)], p_out.at[at(c)], out_sem.at[c, 0]),
                    pltpu.make_async_copy(grad.at[at(c)], g_out.at[at(c)], out_sem.at[c, 1]))

        @pl.loop(0, n_chunks)
        def _(c, s=s):
            dz = z_diff(vz, c, False)
            arrive(2 * s + 1, c)
            div = (x_diff(2 * s + 1, c, vx[at(c), :], xm)
                   + y_diff(2 * s + 1, c, vy[at(c), :], ym) + dz)
            p[padded_at(c), :] = p[padded_at(c), :] - kap[at(c), :] * div

            @pl.when(c == REC_DEPTH // ZC)
            def _():
                row = pad + REC_DEPTH * cx
                p[row:row + cx, :] = p[row:row + cx, :] + inj[s]

            f = p[padded_at(c), :]
            grad[at(c), :] = grad[at(c), :] + fwd[s, at(c), :] * f
            if s < STEPS - 1:
                post(2 * s + 2, c, sxp, f, f)
            else:
                for copy in result(c):
                    copy.start()

    @pl.loop(0, n_chunks)
    def _(c):
        for ph in range(4):
            for d in range(4):
                @pl.when(has[d])
                def _(ph=ph, d=d):
                    halo_copy(ph, c, d).wait_send()

    @pl.loop(1, devices)
    def _(o):
        trace_copy(o).wait_send()

    @pl.loop(0, n_chunks)
    def _(c):
        for copy in result(c):
            copy.wait()

    for copy in outs:
        copy.wait()


def hand_out(n_chunks, p_in, v_in, g_in, p_out, v_out, g_out, sem):
    rows = p_in.shape[0] // n_chunks
    copies = []
    for c in range(n_chunks):
        at = pl.ds(c * rows, rows)
        copies.append(pltpu.make_async_copy(p_in.at[at], p_out.at[at], sem.at[c, 0]))
        copies.append(pltpu.make_async_copy(g_in.at[at], g_out.at[at], sem.at[c, 1]))
        for i in range(3):
            copies.append(pltpu.make_async_copy(v_in.at[i, at], v_out.at[i, at], sem.at[c, 2 + i]))
    for copy in copies:
        copy.start()
    for copy in copies:
        copy.wait()


def local(
    pressure, velocity, kappa, buoyancy, fwd_pressure, gradient, traces, kernel, rec_tile, rec_cell
):
    nz, cx, cy = pressure.shape
    n_rows, samples = traces.shape
    n_tx, n_ty = lax.axis_size("tx"), lax.axis_size("ty")
    devices = n_tx * n_ty
    hbm = pl.BlockSpec(memory_space=pltpu.HBM)
    rows = nz * cx
    cr = ZC * cx
    nc = rows // cr
    pad = 4 * cx
    flat = lambda a: a.reshape(a.shape[:-3] + (rows, cy))
    field = lambda *lead: pltpu.VMEM(lead + (rows, cy), F32)
    half = lambda *shape: pltpu.VMEM(shape, BF16)
    dma = pltpu.SemaphoreType.DMA
    shapes = (jax.ShapeDtypeStruct((rows, cy), F32), jax.ShapeDtypeStruct((3, rows, cy), F32),
              jax.ShapeDtypeStruct((rows, cy), F32))
    results = pl.pallas_call(
        functools.partial(step_kernel, n_tx, n_ty, nz, cx, cy),
        out_shape=shapes,
        in_specs=[hbm] * 10,
        out_specs=(hbm,) * 3,
        scratch_shapes=[
            pltpu.VMEM((rows + 2 * pad, cy), F32), field(), field(),
            pltpu.VMEM((rows + 2 * pad, cy), F32), field(), field(3), field(STEPS), field(),
            pltpu.VMEM((n_rows, samples), F32), pltpu.VMEM(kernel.shape, F32),
            pltpu.VMEM((1, n_rows), jnp.int32), pltpu.VMEM((1, n_rows), jnp.int32),
            half(cr, 3 * cr + 384), half(cr, 3 * cr + 384),
            half(3 * cy + 128, cy), half(3 * cy + 128, cy),
            half(7 * ZC, 2 * cr), half(7 * ZC, 2 * cr), half(16, 2 * cy),
            pltpu.VMEM((4, nc, 7 * ZC, cy), F32), pltpu.VMEM((4, nc, 7 * ZC, cy), F32),
            pltpu.VMEM((4, nc, 16, cr), F32), pltpu.VMEM((4, nc, 16, cr), F32),
            pltpu.VMEM((devices, 8, 128), F32), pltpu.VMEM((devices, 8, 128), F32),
            pltpu.VMEM((STEPS, cx, cy), F32),
            dma((12,)), dma((max(nc, 3), 3)), dma((4, nc, 4)), dma((4, nc, 4)), dma((devices,)), dma((devices,)),
        ],
        compiler_params=pltpu.CompilerParams(
            collective_id=0, has_side_effects=True, vmem_limit_bytes=62 * 2**20),
        name="steps",
    )(flat(pressure), flat(velocity), flat(kappa), flat(buoyancy), flat(fwd_pressure),
      flat(gradient), traces, kernel, rec_tile.reshape(1, n_rows), rec_cell.reshape(1, n_rows))
    press, vel, grad = pl.pallas_call(
        functools.partial(hand_out, nc),
        out_shape=shapes,
        in_specs=[hbm] * 3,
        out_specs=(hbm,) * 3,
        scratch_shapes=[dma((nc, 5))],
        compiler_params=pltpu.CompilerParams(vmem_limit_bytes=62 * 2**20),
        name="hand_out",
    )(*results)
    return (press.reshape(nz, cx, cy), vel.reshape(3, nz, cx, cy), grad.reshape(nz, cx, cy))


def solution(mesh):
    return jax.shard_map(
        local,
        mesh=mesh,
        in_specs=(
            P(None, "tx", "ty"),
            P(None, None, "tx", "ty"),
            P(None, "tx", "ty"),
            P(None, None, "tx", "ty"),
            P(None, None, "tx", "ty"),
            P(None, "tx", "ty"),
            P(("tx", "ty"), None),
            P(),
            P(("tx", "ty"), None),
            P(("tx", "ty")),
        ),
        out_specs=(P(None, "tx", "ty"), P(None, None, "tx", "ty"), P(None, "tx", "ty")),
        check_vma=False,
    )
```

```python
import functools

import jax
import jax.numpy as jnp
import ml_dtypes
import numpy as np
from jax import lax
from jax.experimental import pallas as pl
from jax.experimental.pallas import tpu as pltpu
from jax.sharding import PartitionSpec as P

STEPS = 2
REC_DEPTH = 3
ZC = 16
MESH = pl.DeviceIdType.MESH
F32 = jnp.float32
BF16 = jnp.bfloat16

coeffs = (1225.0 / 1024.0, -245.0 / 3072.0, 49.0 / 5120.0, -5.0 / 7168.0)


def tap(offset, plus):
    for k in range(1, 5):
        if offset == (k if plus else k - 1):
            return coeffs[k - 1]
        if offset == (1 - k if plus else -k):
            return -coeffs[k - 1]
    return 0.0


def taps(offset, plus):
    hi = jnp.zeros(offset.shape, F32)
    lo = jnp.zeros(offset.shape, F32)
    for at in range(-4, 5):
        c = tap(at, plus)
        if c != 0.0:
            c_hi = float(np.float32(c).astype(ml_dtypes.bfloat16))
            hi = jnp.where(offset == at, c_hi, hi)
            lo = jnp.where(offset == at, float(np.float32(c)) - c_hi, lo)
    return hi, lo


def grid_of(shape):
    return (lax.broadcasted_iota(jnp.int32, shape, 0), lax.broadcasted_iota(jnp.int32, shape, 1))


FAR = 1 << 20


def log2(n):
    return n.bit_length() - 1


def build_x(ref, cx, plus):
    cr = ZC * cx
    low = 3 if plus else 4
    row, col = grid_of((cr, cr))
    sx, mx = log2(cx), cx - 1
    hi, lo = taps(jnp.where(row >> sx == col >> sx, (col & mx) - (row & mx), FAR), plus)
    ref[:, 0:cr] = hi.astype(BF16)
    ref[:, cr:2 * cr] = hi.astype(BF16)
    ref[:, 2 * cr:3 * cr] = lo.astype(BF16)
    row, col = grid_of((cr, 128))
    layer = col >> log2(ZC)
    x = jnp.where(layer < low, layer - low, cx + layer - low)
    near = (row >> sx == col & (ZC - 1)) & (layer < 7)
    hi, lo = taps(jnp.where(near, x - (row & mx), FAR), plus)
    ref[:, 3 * cr:3 * cr + 128] = hi.astype(BF16)
    ref[:, 3 * cr + 128:3 * cr + 256] = hi.astype(BF16)
    ref[:, 3 * cr + 256:] = lo.astype(BF16)


def build_y(ref, cy, plus):
    row, col = grid_of((cy, cy))
    hi, lo = taps(row - col, plus)
    ref[0:cy] = hi.astype(BF16)
    ref[cy:2 * cy] = hi.astype(BF16)
    ref[2 * cy:3 * cy] = lo.astype(BF16)
    row, col = grid_of((ref.shape[0] - 3 * cy, cy))
    seg, at = row >> 4, row & 15
    hi, lo = taps(jnp.where(at < 8, at - 8, cy + at - 8) - col, plus)
    ref[3 * cy:] = jnp.where(seg < 2, hi, jnp.where(seg == 2, lo, 0.0)).astype(BF16)


def build_x_edges(ref, cx, plus):
    low = 3 if plus else 4
    row, col = grid_of(ref.shape)
    at = col & (ZC * cx - 1)
    layer = row >> log2(ZC)
    x = jnp.where(layer < low, cx - low + layer, layer - low)
    ref[...] = jnp.where(at == (row & (ZC - 1)) * cx + x, 1.0, 0.0).astype(BF16)


def split(v):
    hi = v.astype(BF16)
    return hi, (v - hi.astype(F32)).astype(BF16)


def dot(a, b):
    return lax.dot_general(a, b, (((1,), (0,)), ((), ())), preferred_element_type=F32)


def dot_nt(a, b):
    return lax.dot_general(a, b, (((1,), (1,)), ((), ())), preferred_element_type=F32)


def pack(devices, traces, kernel, tiles, cells):
    rows = traces.shape[0]
    src = lax.dot_general(
        kernel, traces, (((1,), (1,)), ((), ())),
        precision=lax.Precision.HIGHEST, preferred_element_type=F32)
    named = lax.broadcasted_iota(jnp.int32, (devices, rows), 0) == tiles
    onehot = jnp.where(named, 1.0, 0.0)
    row, col = grid_of((rows, rows))
    count = dot(onehot.astype(BF16), jnp.where(row < col, 1.0, 0.0).astype(BF16))
    rank = jnp.sum(count * onehot, axis=0, keepdims=True)
    slot_id = lax.broadcasted_iota(jnp.int32, (128, rows), 0).astype(F32)
    place = jnp.where(slot_id == rank, 1.0, 0.0).astype(BF16)
    src_hi = src.astype(BF16).astype(F32)
    cell_lo = cells % 256
    none = jnp.zeros((5, rows), F32)
    hi = jnp.concatenate([src_hi, (cells - cell_lo).astype(F32), none], axis=0)
    lo = jnp.concatenate([src - src_hi, cell_lo.astype(F32), none], axis=0)
    packed = None
    for v in (hi, lo):
        spread = jnp.concatenate([v] * devices, axis=0)
        to = lax.broadcasted_iota(jnp.int32, (devices * 8, rows), 0) >> 3 == tiles
        part = dot_nt(jnp.where(to, spread, 0.0).astype(BF16), place)
        packed = part if packed is None else packed + part
    return packed.reshape(devices, 8, 128)


def step_kernel(n_tx, n_ty, nz, cx, cy,
                p_in, v_in, kap_in, b_in, fwd_in, g_in, traces_in, kernel_in, tile_in, cell_in,
                p_out, v_out, g_out,
                p, vx, vy, vz, kap, buo, fwd, grad, traces, filt, tiles, cells,
                xp, xm, yp, ym, sxp, sxm,
                xs, xr, ys, yr, ts, tr, inj,
                in_sem, out_sem, send_sem, recv_sem, to_sem, from_sem):
    tx, ty = lax.axis_index("tx"), lax.axis_index("ty")
    devices = n_tx * n_ty
    me = tx * n_ty + ty
    rows = nz * cx
    cr = ZC * cx
    pad = 4 * cx
    n_chunks = rows // cr
    has = (tx < n_tx - 1, tx > 0, ty < n_ty - 1, ty > 0)
    ids = ({"tx": tx + 1}, {"tx": tx - 1}, {"ty": ty + 1}, {"ty": ty - 1})
    back = (1, 0, 3, 2)

    body = pl.ds(pad, rows)
    pairs = [
        (p_in, p.at[body]), (traces_in, traces), (kernel_in, filt), (tile_in, tiles),
        (cell_in, cells), (v_in.at[0], vx), (v_in.at[1], vy), (v_in.at[2], vz.at[body]),
        (b_in, buo), (kap_in, kap), (fwd_in, fwd), (g_in, grad),
    ]
    loads = [pltpu.make_async_copy(a, b, in_sem.at[i]) for i, (a, b) in enumerate(pairs)]
    for copy in loads:
        copy.start()

    barrier = pltpu.get_barrier_semaphore()

    def peer(o):
        to = lax.rem(me + o, devices)
        return to, {"tx": to // n_ty, "ty": lax.rem(to, n_ty)}

    @pl.loop(1, devices)
    def _(o):
        pl.semaphore_signal(barrier, inc=1, device_id=peer(o)[1], device_id_type=MESH)

    zeros = jnp.zeros((pad, cy), F32)
    for ref in (p, vz):
        ref[0:pad, :] = zeros
        ref[pad + rows:, :] = zeros

    def span(ph, d):
        low, up = (3 * ZC, 4 * ZC) if ph % 2 == 0 else (4 * ZC, 3 * ZC)
        return ((0, low), (low, up), (0, 8), (8, 8))[d]

    def clear(d):
        @pl.when(jnp.logical_not(has[back[d]]))
        def _():
            for ph in range(4):
                start, size = span(ph, d)
                ref = xr if d < 2 else yr
                for c in range(n_chunks):
                    ref[ph, c, start:start + size, :] = jnp.zeros((size, ref.shape[3]), F32)

    for d in range(4):
        clear(d)

    build_x_edges(sxp, cx, True)
    pl.semaphore_wait(barrier, devices - 1)

    def halo_copy(ph, c, d):
        start, size = span(ph, d)
        src, dst = (xs, xr) if d < 2 else (ys, yr)
        return pltpu.make_async_remote_copy(
            src_ref=src.at[ph, c, pl.ds(start, size)],
            dst_ref=dst.at[ph, c, pl.ds(start, size)],
            send_sem=send_sem.at[ph, c, d],
            recv_sem=recv_sem.at[ph, c, d],
            device_id=ids[d], device_id_type=MESH)

    def send(ph, c):
        for d in range(4):
            @pl.when(has[d])
            def _(d=d):
                halo_copy(ph, c, d).start()

    def arrive(ph, c):
        for d in range(4):
            @pl.when(has[back[d]])
            def _(d=d):
                start, size = span(ph, d)
                src, dst = (xs, xr) if d < 2 else (ys, yr)
                pltpu.make_async_remote_copy(
                    src_ref=src.at[ph, c, pl.ds(start, size)],
                    dst_ref=dst.at[ph, c, pl.ds(start, size)],
                    send_sem=send_sem.at[ph, c, d],
                    recv_sem=recv_sem.at[ph, c, d],
                    device_id=ids[back[d]], device_id_type=MESH).wait_recv()

    def post(ph, c, pick, fx, fy):
        hi, lo = split(fx)
        xs[ph, c] = dot(pick[...], jnp.concatenate([hi, lo], axis=0))
        lane = lax.broadcasted_iota(jnp.int32, (cr, 128), 1)
        turned = jnp.where(lane < 8, fy[:, 0:128], fy[:, cy - 128:cy]).T
        ys[ph, c] = jnp.concatenate([turned[120:128], turned[0:8]], axis=0)
        send(ph, c)

    def x_diff(ph, c, field, matrix):
        hi, lo = split(field)
        hh, hl = split(xr[ph, c])
        gap = jnp.zeros((16, cy), BF16)
        return dot(matrix[...], jnp.concatenate([hi, lo, hi, hh, gap, hl, gap, hh, gap], axis=0))

    def y_diff(ph, c, field, matrix):
        hi, lo = split(field)
        hh, hl = split(yr[ph, c])
        hh, hl = hh.astype(F32), hl.astype(F32)
        halo = jnp.concatenate([hh, hl, hh, jnp.zeros((80, cr), F32)], axis=0)
        return dot(jnp.concatenate([hi, lo, hi, halo.T.astype(BF16)], axis=1), matrix[...])

    def z_diff(ref, c, plus):
        total = None
        for k in range(1, 5):
            a, b = (k, 1 - k) if plus else (k - 1, -k)
            fa = ref[pl.ds(pl.multiple_of(c * cr + (pad + a * cx), 8), cr), :]
            fb = ref[pl.ds(pl.multiple_of(c * cr + (pad + b * cx), 8), cr), :]
            term = coeffs[k - 1] * (fa - fb)
            total = term if total is None else total + term
        return total

    def at(c):
        return pl.ds(pl.multiple_of(c * cr, cr), cr)

    def padded_at(c):
        return pl.ds(pl.multiple_of(c * cr + pad, 8), cr)

    loads[0].wait()

    @pl.loop(0, n_chunks)
    def _(c):
        f = p[padded_at(c), :]
        post(0, c, sxp, f, f)

    def trace_copy(o):
        to, place = peer(o)
        return pltpu.make_async_remote_copy(
            src_ref=ts.at[to], dst_ref=tr.at[o],
            send_sem=to_sem.at[o], recv_sem=from_sem.at[o],
            device_id=place, device_id_type=MESH)

    for i in range(1, 5):
        loads[i].wait()
    ts[...] = pack(devices, traces[...], filt[...], tiles[...], cells[...])

    @pl.loop(1, devices)
    def _(o):
        trace_copy(o).start()

    tr[0] = ts[me]
    build_x(xp, cx, True)
    build_y(yp, cy, True)
    build_x_edges(sxm, cx, False)
    for i in range(5, 9):
        loads[i].wait()

    def receive():
        @pl.loop(1, devices)
        def _(o):
            trace_copy(o).wait_recv()

        def gather(i, total):
            got = jnp.concatenate([tr[4 * i + j] for j in range(4)], axis=1)
            cell = got[2:3].astype(jnp.int32)
            at_x = lax.broadcasted_iota(jnp.int32, (cx, 512), 0) == cell // cy
            at_y = lax.broadcasted_iota(jnp.int32, (cy, 512), 0) == cell % cy
            pieces = []
            for s in range(STEPS):
                v = got[s:s + 1]
                hi = v.astype(BF16).astype(F32)
                pieces.append(jnp.where(at_x, hi, 0.0).astype(BF16))
                pieces.append(jnp.where(at_x, v - hi, 0.0).astype(BF16))
            return total + dot_nt(jnp.concatenate(pieces, axis=0),
                                  jnp.where(at_y, 1.0, 0.0).astype(BF16))

        total = lax.fori_loop(0, devices // 4, gather, jnp.zeros((4 * cx, cy), F32))
        for s in range(STEPS):
            inj[s] = total[2 * s * cx:(2 * s + 1) * cx] + total[(2 * s + 1) * cx:(2 * s + 2) * cx]

    for s in range(STEPS):
        @pl.loop(0, n_chunks)
        def _(c, s=s):
            nz_new = vz[padded_at(c), :] - buo[2, at(c), :] * z_diff(p, c, True)
            vz[padded_at(c), :] = nz_new
            arrive(2 * s, c)
            f = p[padded_at(c), :]
            nx = vx[at(c), :] - buo[0, at(c), :] * x_diff(2 * s, c, f, xp)
            vx[at(c), :] = nx
            ny = vy[at(c), :] - buo[1, at(c), :] * y_diff(2 * s, c, f, yp)
            vy[at(c), :] = ny
            post(2 * s + 1, c, sxm, nx, ny)

        if s == 0:
            build_x(xm, cx, False)
            build_y(ym, cy, False)
            receive()
            for i in range(9, 12):
                loads[i].wait()

        if s == STEPS - 1:
            outs = [
                pltpu.make_async_copy(vx, v_out.at[0], out_sem.at[0, 2]),
                pltpu.make_async_copy(vy, v_out.at[1], out_sem.at[1, 2]),
                pltpu.make_async_copy(vz.at[body], v_out.at[2], out_sem.at[2, 2]),
            ]
            for copy in outs:
                copy.start()

        def result(c):
            return (pltpu.make_async_copy(p.at[padded_at(c)], p_out.at[at(c)], out_sem.at[c, 0]),
                    pltpu.make_async_copy(grad.at[at(c)], g_out.at[at(c)], out_sem.at[c, 1]))

        @pl.loop(0, n_chunks)
        def _(c, s=s):
            dz = z_diff(vz, c, False)
            arrive(2 * s + 1, c)
            div = (x_diff(2 * s + 1, c, vx[at(c), :], xm)
                   + y_diff(2 * s + 1, c, vy[at(c), :], ym) + dz)
            p[padded_at(c), :] = p[padded_at(c), :] - kap[at(c), :] * div

            @pl.when(c == REC_DEPTH // ZC)
            def _():
                row = pad + REC_DEPTH * cx
                p[row:row + cx, :] = p[row:row + cx, :] + inj[s]

            f = p[padded_at(c), :]
            grad[at(c), :] = grad[at(c), :] + fwd[s, at(c), :] * f
            if s < STEPS - 1:
                post(2 * s + 2, c, sxp, f, f)
            else:
                for copy in result(c):
                    copy.start()

    @pl.loop(0, n_chunks)
    def _(c):
        for ph in range(4):
            for d in range(4):
                @pl.when(has[d])
                def _(ph=ph, d=d):
                    halo_copy(ph, c, d).wait_send()

    @pl.loop(1, devices)
    def _(o):
        trace_copy(o).wait_send()

    @pl.loop(0, n_chunks)
    def _(c):
        for copy in result(c):
            copy.wait()

    for copy in outs:
        copy.wait()


def hand_out(n_chunks, p_in, v_in, g_in, p_out, v_out, g_out, held, sem_in, sem_out):
    rows = p_in.shape[0] // n_chunks
    reads, writes = [], []
    for c in range(n_chunks):
        at = pl.ds(c * rows, rows)
        ends = [(p_in.at[at], p_out.at[at]), (g_in.at[at], g_out.at[at])]
        ends += [(v_in.at[i, at], v_out.at[i, at]) for i in range(3)]
        for i, (a, b) in enumerate(ends):
            reads.append(pltpu.make_async_copy(a, held.at[i, at], sem_in.at[c, i]))
            writes.append(pltpu.make_async_copy(held.at[i, at], b, sem_out.at[c, i]))
    for copy in reads:
        copy.start()
    for read, write in zip(reads, writes):
        read.wait()
        write.start()
    for copy in writes:
        copy.wait()


def local(
    pressure, velocity, kappa, buoyancy, fwd_pressure, gradient, traces, kernel, rec_tile, rec_cell
):
    nz, cx, cy = pressure.shape
    n_rows, samples = traces.shape
    n_tx, n_ty = lax.axis_size("tx"), lax.axis_size("ty")
    devices = n_tx * n_ty
    hbm = pl.BlockSpec(memory_space=pltpu.HBM)
    rows = nz * cx
    cr = ZC * cx
    nc = rows // cr
    pad = 4 * cx
    flat = lambda a: a.reshape(a.shape[:-3] + (rows, cy))
    field = lambda *lead: pltpu.VMEM(lead + (rows, cy), F32)
    half = lambda *shape: pltpu.VMEM(shape, BF16)
    dma = pltpu.SemaphoreType.DMA
    shapes = (jax.ShapeDtypeStruct((rows, cy), F32), jax.ShapeDtypeStruct((3, rows, cy), F32),
              jax.ShapeDtypeStruct((rows, cy), F32))
    results = pl.pallas_call(
        functools.partial(step_kernel, n_tx, n_ty, nz, cx, cy),
        out_shape=shapes,
        in_specs=[hbm] * 10,
        out_specs=(hbm,) * 3,
        scratch_shapes=[
            pltpu.VMEM((rows + 2 * pad, cy), F32), field(), field(),
            pltpu.VMEM((rows + 2 * pad, cy), F32), field(), field(3), field(STEPS), field(),
            pltpu.VMEM((n_rows, samples), F32), pltpu.VMEM(kernel.shape, F32),
            pltpu.VMEM((1, n_rows), jnp.int32), pltpu.VMEM((1, n_rows), jnp.int32),
            half(cr, 3 * cr + 384), half(cr, 3 * cr + 384),
            half(3 * cy + 128, cy), half(3 * cy + 128, cy),
            half(7 * ZC, 2 * cr), half(7 * ZC, 2 * cr),
            pltpu.VMEM((4, nc, 7 * ZC, cy), F32), pltpu.VMEM((4, nc, 7 * ZC, cy), F32),
            pltpu.VMEM((4, nc, 16, cr), F32), pltpu.VMEM((4, nc, 16, cr), F32),
            pltpu.VMEM((devices, 8, 128), F32), pltpu.VMEM((devices, 8, 128), F32),
            pltpu.VMEM((STEPS, cx, cy), F32),
            dma((12,)), dma((max(nc, 3), 3)), dma((4, nc, 4)), dma((4, nc, 4)), dma((devices,)), dma((devices,)),
        ],
        compiler_params=pltpu.CompilerParams(
            collective_id=0, has_side_effects=True, vmem_limit_bytes=62 * 2**20),
        name="steps",
    )(flat(pressure), flat(velocity), flat(kappa), flat(buoyancy), flat(fwd_pressure),
      flat(gradient), traces, kernel, rec_tile.reshape(1, n_rows), rec_cell.reshape(1, n_rows))
    press, vel, grad = pl.pallas_call(
        functools.partial(hand_out, nc),
        out_shape=shapes,
        in_specs=[hbm] * 3,
        out_specs=(hbm,) * 3,
        scratch_shapes=[field(5), dma((nc, 5)), dma((nc, 5))],
        compiler_params=pltpu.CompilerParams(vmem_limit_bytes=62 * 2**20),
        name="hand_out",
    )(*results)
    return (press.reshape(nz, cx, cy), vel.reshape(3, nz, cx, cy), grad.reshape(nz, cx, cy))


def solution(mesh):
    return jax.shard_map(
        local,
        mesh=mesh,
        in_specs=(
            P(None, "tx", "ty"),
            P(None, None, "tx", "ty"),
            P(None, "tx", "ty"),
            P(None, None, "tx", "ty"),
            P(None, None, "tx", "ty"),
            P(None, "tx", "ty"),
            P(("tx", "ty"), None),
            P(),
            P(("tx", "ty"), None),
            P(("tx", "ty")),
        ),
        out_specs=(P(None, "tx", "ty"), P(None, None, "tx", "ty"), P(None, "tx", "ty")),
        check_vma=False,
    )
```
